32 devices in a mesh: blk: 8 (over z, x), leaf: 4 (over y, core).
Axes of the slice: x: 2, y: 2, z: 4, core: 2. Of those that a mesh axis runs over, the one named last changes fastest.
Arguments:
- columns_in: bfloat16 [8, 4, 8192, 512], P('blk', 'leaf'), may hold values from -6 to 6
- leaf_basis: bfloat16 [8, 4, 64, 128, 128], P('blk', 'leaf'), may hold values from -0.5 to 0.5
- transfers: bfloat16 [8, 8, 4, 64, 128, 256], P('blk', None, 'leaf'), may hold values from -0.4375 to 0.4375
- row_basis: bfloat16 [8, 4, 64, 128, 128], P('blk', 'leaf'), may hold values from -0.21875 to 0.21875
- ranks: int32 [8, 9, 4, 64], P('blk', None, 'leaf'), may hold values from 64 to 128, as said below
- col_owner: int32 [4], replicated, may hold values from 0 to 3, each once
- row_owner: int32 [4], replicated, may hold values from 0 to 3, each once
Outputs:
- row_sums: bfloat16 [4, 8192, 512], P('leaf', 'blk')
The draws below stay inside these ranges and needn't reach their ends.
Inputs may be any that keep to these rules, and one draw needn't show every extreme that they name: ranks of every node of every level; the smallest and the largest value each occur. `col_owner`: each subtree number once. `row_owner`: each subtree number once.
All inputs are finite; a program needn't handle non-finite values.
Results may differ from the reference program's by a relative error of at most 0.019.
Values may be sent and summed in bfloat16 or wider, within the bound.
No kernel may reach another device: no remote copies, remote signals or barrier semaphores. Data moves between devices by JAX's collectives and lax.ppermute only.
A program may use at most 192 MiB of HBM per device.

```python
import jax
import jax.numpy as jnp
from jax import lax

LEAF = 128
R = 128
LEVELS = 8
RHS = 512
MID = 4
OWNERS = 4
BLOCKS = 8
NODES_DEV = 64
SUB = 8192


def draw_ranks(key, part):
    shape = (BLOCKS, LEVELS + 1, OWNERS, NODES_DEV)
    base = jax.random.randint(key, shape, R // 2, R + 1).astype(jnp.int32)
    flat = base.reshape(-1)
    count = flat.shape[0]
    first = jax.random.randint(jax.random.fold_in(key, 11), (), 0, count)
    offset = jax.random.randint(jax.random.fold_in(key, 12), (), 1, count)
    second = (first + offset) % count
    flat = flat.at[first].set(R).at[second].set(R // 2)
    return flat.reshape(shape).astype(jnp.int32)


def block_levels(own_key, extent, split, smallest, largest):
    def one(dim, blocks):
        draws = jax.random.uniform(jax.random.fold_in(jax.random.fold_in(own_key, 6), dim), (blocks,), jnp.float32, smallest / len(split), largest / len(split))
        return jnp.repeat(jnp.exp(draws), extent[dim] // blocks).reshape((-1,) + (1,) * (len(extent) - dim - 1))

    level = one(*split[0])
    for cut in split[1:]:
        level = level * one(*cut)
    return level


def noise(key, extent, width, most, pieces=(), held_as=jnp.bfloat16):
    drawn = width * jax.random.normal(key, extent, jnp.float32)
    if pieces:
        drawn = drawn * block_levels(key, extent, pieces, -0.22, 0.18)
    return jnp.clip(drawn, -most, most).astype(held_as)


def setup_inputs(seed: int = 0) -> dict:
    seeds = jax.random.split(jax.random.key(seed), 8)
    return {
        "columns_in": noise(seeds[0], (BLOCKS, OWNERS, SUB, RHS), 1.0, 6.0, ((0, 8), (1, 4))),
        "leaf_basis": noise(seeds[1], (BLOCKS, OWNERS, NODES_DEV, LEAF, R), LEAF ** -0.5, 0.5, ((0, 8), (1, 4))),
        "transfers": noise(seeds[2], (BLOCKS, LEVELS, OWNERS, NODES_DEV, R, 2 * R), (3 * R // 2) ** -0.5, 0.4375, ((0, 8), (2, 4))),
        "row_basis": noise(seeds[3], (BLOCKS, OWNERS, NODES_DEV, LEAF, R), (3 * R * BLOCKS // 4) ** -0.5, 0.21875, ((0, 8), (1, 4))),
        "ranks": draw_ranks(jax.random.fold_in(seeds[7], 71), 0),
        "col_owner": jax.random.permutation(seeds[5], OWNERS).astype(jnp.int32),
        "row_owner": jax.random.permutation(seeds[6], OWNERS).astype(jnp.int32),
    }


def apply_ranks(coeffs, live):
    row_ids = jnp.arange(coeffs.shape[-2], dtype=jnp.int32)
    keep = (row_ids[:, None] < live[..., None, None]).astype(jnp.float32)
    return coeffs * keep


def one_block(inputs, leaf_basis, transfers, row_basis, ranks, col_owner, row_owner):
    owners = OWNERS
    nodes_local = NODES_DEV
    values = inputs.reshape(owners, nodes_local, LEAF, RHS).astype(jnp.float32)
    current = jnp.einsum('onlr,onlh->onrh', leaf_basis.astype(jnp.float32), values)
    coeffs = apply_ranks(current, ranks[0]).astype(jnp.bfloat16)
    for level_index in range(1, MID + 1):
        half_j = 2 ** (LEVELS - level_index) // owners
        half_i = 2 ** (level_index - 1)
        previous = coeffs.astype(jnp.float32).reshape(owners, half_j, 2, half_i, R, RHS)
        mixing = transfers[level_index - 1].astype(jnp.float32).reshape(owners, half_j, half_i, 2, R, 2, R)
        live = ranks[level_index]
        if level_index < MID:
            current = jnp.einsum('ojibrtq,ojtiqh->ojibrh', mixing, previous)
        else:
            current = jnp.einsum('ojibrtq,ojtiqh->oibjrh', mixing, previous)
            live = live.reshape(owners, half_j, half_i, 2).transpose(0, 2, 3, 1)
        coeffs = apply_ranks(current.reshape(owners, nodes_local, R, RHS), live.reshape(owners, nodes_local)).astype(jnp.bfloat16)
    sub_i = 2 ** MID // owners
    part_j = 2 ** (LEVELS - MID) // owners
    grouped = coeffs.reshape(owners, owners, sub_i, part_j, R, RHS)
    outgoing = jnp.take(grouped, row_owner.astype(jnp.int32), axis=1)
    incoming = jnp.transpose(outgoing, (1, 2, 0, 3, 4, 5))
    inverse = jnp.argsort(col_owner).astype(jnp.int32)
    coeffs = jnp.take(incoming, inverse, axis=2).reshape(owners, nodes_local, R, RHS)
    for level_index in range(MID + 1, LEVELS + 1):
        half_i = 2 ** (level_index - 1) // owners
        half_j = 2 ** (LEVELS - level_index)
        previous = coeffs.astype(jnp.float32).reshape(owners, half_i, half_j, 2, R, RHS)
        mixing = transfers[level_index - 1].astype(jnp.float32).reshape(owners, half_i, 2, half_j, R, 2, R)
        current = jnp.einsum('oibjrtq,oijtqh->oibjrh', mixing, previous)
        coeffs = apply_ranks(current.reshape(owners, nodes_local, R, RHS), ranks[level_index]).astype(jnp.bfloat16)
    result = jnp.einsum('onlr,onrh->onlh', row_basis.astype(jnp.float32), coeffs.astype(jnp.float32))
    return result.reshape(owners, SUB, RHS)


def reference(columns_in, leaf_basis, transfers, row_basis, ranks, col_owner, row_owner):
    def add_block(total, items):
        inputs, leaves, mixers, rows_basis, rank_table = items
        return total + one_block(inputs, leaves, mixers, rows_basis, rank_table, col_owner, row_owner), None

    start_total = jnp.zeros((OWNERS, SUB, RHS), jnp.float32)
    total, unused = lax.scan(add_block, start_total, (columns_in, leaf_basis, transfers, row_basis, ranks))
    return total.astype(jnp.bfloat16)
```

```python
import functools

import jax
import jax.numpy as jnp
from jax import lax
from jax.experimental import pallas as pl
from jax.experimental.pallas import tpu as pltpu
from jax.sharding import PartitionSpec as P

F32 = jnp.float32
BF16 = jnp.bfloat16
VMEM_LIMIT = 56 * 2**20
UNROLL = 4
COST = 1
IN_FLIGHT = 1
CHUNKS = ((128, 1), (128, 3))


def put_masked(ref, index, value, rank):
    width = value.shape[0]
    half = width // 2
    ref[(*index, slice(0, half))] = value[:half].astype(BF16)
    rows = lax.broadcasted_iota(jnp.int32, (half, value.shape[1]), 0) + half
    ref[(*index, slice(half, width))] = jnp.where(rows < rank, value[half:], 0.0).astype(BF16)


def over_trees(trees, body):
    step = min(UNROLL, trees)

    def group(g, carry):
        for u in range(step):
            body(g * step + u)
        return carry

    if step == trees:
        group(0, 0)
    else:
        lax.fori_loop(0, trees // step, group, 0)


def column_kernel(sizes, start, meta, row_owner, ranks, columns_in, leaf_basis, mixings, *rest):
    owners, half_levels, tree, nodes, width = sizes
    outs, (ping, pong, cols, leaf, mix, arrived) = rest[:-6], rest[-6:]
    chunks = len(outs)
    part = outs[0].shape[-1]
    trees = nodes // tree
    copies = [
        pltpu.make_async_copy(leaf_basis.at[0, 0], leaf, arrived.at[0]),
        pltpu.make_async_copy(columns_in.at[0, 0, :, pl.ds(start, cols.shape[1])], cols, arrived.at[1]),
    ] + [
        pltpu.make_async_copy(mixings.at[0, level, 0], mix.at[level], arrived.at[2 + level])
        for level in range(half_levels)
    ]
    for copy in copies:
        copy.start()
    copies[0].wait()
    copies[1].wait()

    def leaves(j):
        for n in range(tree):
            node = j * tree + n
            rows = cols[pl.ds(pl.multiple_of(node * width, width), width), :]
            value = lax.dot_general(leaf[node], rows, (((0,), (0,)), ((), ())), preferred_element_type=F32)
            put_masked(ping, (node,), value, ranks[node])

    over_trees(trees, leaves)
    now, later = ping, pong
    for level in range(1, half_levels):
        copies[1 + level].wait()
        half_i = 2 ** (level - 1)

        def mixed(j, now=now, later=later, level=level, half_i=half_i):
            for jj in range(tree // (2 * half_i)):
                for i in range(half_i):
                    first = j * tree + jj * 2 * half_i
                    x = jnp.concatenate([now[first + i], now[first + half_i + i]], axis=0)
                    n = first + 2 * i
                    t = mix[level - 1, pl.ds(n, 2)].reshape(2 * width, 2 * width)
                    value = jnp.dot(t, x, preferred_element_type=F32)
                    for e in range(2):
                        rank = ranks[level * nodes + n + e]
                        put_masked(later, (n + e,), value[e * width : (e + 1) * width], rank)

        over_trees(trees, mixed)
        now, later = later, now
    copies[1 + half_levels].wait()
    half_i = tree // 2
    pairs = half_i // owners

    def last(j):
        for d in range(owners):
            target = row_owner[d]
            for p in range(pairs):
                i = target * pairs + p
                first = j * tree + i
                x = jnp.concatenate([now[first], now[first + half_i]], axis=0)
                n = j * tree + 2 * i
                t = mix[half_levels - 1, pl.ds(n, 2)].reshape(2 * width, 2 * width)
                value = jnp.dot(t, x, preferred_element_type=F32)
                for e in range(2):
                    rank = ranks[half_levels * nodes + n + e]
                    v = value[e * width : (e + 1) * width]
                    for c in range(chunks):
                        put_masked(outs[c], (d, 2 * p + e, j), v[:, c * part : (c + 1) * part], rank)

    over_trees(trees, last)


def row_kernel(sizes, meta, col_owner, ranks, received, mixings, row_basis, *rest):
    owners, half_levels, tree, nodes, width, inner, per_dest = sizes
    outs, (ping, pong, basis, mix, arrived) = rest[:-5], rest[-5:]
    trees = nodes // tree
    copies = [
        pltpu.make_async_copy(mixings.at[0, half_levels + level, 0], mix.at[level], arrived.at[level])
        for level in range(half_levels)
    ] + [pltpu.make_async_copy(row_basis.at[0, 0], basis, arrived.at[half_levels])]
    for copy in copies:
        copy.start()
    copies[0].wait()
    now, later = ping, pong
    half_j = tree // 2
    pairs = half_j // owners

    def first_mixed(p):
        for d in range(owners):
            source = col_owner[d]
            for q in range(pairs):
                n = p * tree + source * pairs + q
                x = received[d, p, 2 * q : 2 * q + 2].reshape(2 * width, -1)
                t = jnp.concatenate([mix[0, n], mix[0, n + half_j]], axis=0)
                value = jnp.dot(t, x, preferred_element_type=F32)
                for e in range(2):
                    m = n + e * half_j
                    rank = ranks[(half_levels + 1) * nodes + m]
                    put_masked(pong, (m,), value[e * width : (e + 1) * width], rank)

    over_trees(trees, first_mixed)
    now, later = later, now
    for level in range(1, half_levels):
        copies[level].wait()
        half_j = tree // 2 ** (level + 1)

        def mixed(p, now=now, later=later, level=level, half_j=half_j):
            for i in range(2**level):
                for j in range(half_j):
                    first = p * tree + i * 2 * half_j
                    x = now[pl.ds(first + 2 * j, 2)].reshape(2 * width, -1)
                    t = jnp.concatenate([mix[level, first + j], mix[level, first + half_j + j]], axis=0)
                    value = jnp.dot(t, x, preferred_element_type=F32)
                    for e in range(2):
                        n = first + e * half_j + j
                        rank = ranks[(half_levels + 1 + level) * nodes + n]
                        put_masked(later, (n,), value[e * width : (e + 1) * width], rank)

        over_trees(trees, mixed)
        now, later = later, now
    copies[half_levels].wait()
    dests = tree // (inner * per_dest)

    def rows(p):
        for e in range(inner):
            lane = meta[0] ^ e
            for z in range(dests):
                for m in range(per_dest):
                    n = p * tree + (z * inner + lane) * per_dest + m
                    value = jnp.dot(basis[n], now[n], preferred_element_type=F32)
                    outs[e][p * dests + z, m * width : (m + 1) * width, :] = value.astype(BF16)

    over_trees(trees, rows)


def local(chunk_groups, inner, columns_in, leaf_basis, transfers, row_basis, ranks, col_owner, row_owner):
    owners = lax.axis_size("leaf")
    blocks = lax.axis_size("blk")
    outer = blocks // inner
    levels = transfers.shape[1]
    half_levels = levels // 2
    nodes, width = leaf_basis.shape[2], leaf_basis.shape[4]
    sides = columns_in.shape[3]
    tree = 2**half_levels
    part_j = nodes // tree
    sub_i = tree // owners
    share = nodes * width // blocks
    per_dest = share // width
    blk = lax.axis_index("blk")
    meta = jnp.stack([blk % inner, blk // inner]).astype(jnp.int32)
    flat_ranks = ranks.reshape(-1)

    mix_scratch = pltpu.VMEM((half_levels, nodes, width, 2 * width), BF16)
    basis_scratch = pltpu.VMEM((nodes, width, width), BF16)
    in_hbm = pl.BlockSpec(memory_space=pl.ANY)
    in_vmem = pl.BlockSpec(memory_space=pltpu.VMEM)
    in_smem = pl.BlockSpec(memory_space=pltpu.SMEM)

    def cost(sides):
        return pl.CostEstimate(flops=int(COST * 5e7 * max(sides, 256)), bytes_accessed=int(COST * 2e7), transcendentals=0)

    def column_half(start, part, chunks, order):
        total = part * chunks
        return pl.pallas_call(
            functools.partial(column_kernel, (owners, half_levels, tree, nodes, width), start),
            in_specs=[in_smem] * 3 + [in_hbm] * 3,
            out_specs=[in_vmem] * chunks,
            scratch_shapes=[pltpu.VMEM((nodes, width, total), BF16)] * 2
            + [
                pltpu.VMEM((nodes * width, total), BF16),
                basis_scratch,
                mix_scratch,
                pltpu.SemaphoreType.DMA((half_levels + 2,)),
            ],
            out_shape=[jax.ShapeDtypeStruct((owners, sub_i, part_j, width, part), BF16)] * chunks,
            compiler_params=pltpu.CompilerParams(vmem_limit_bytes=VMEM_LIMIT),
            cost_estimate=cost(total),
        )(order, row_owner, flat_ranks, columns_in, leaf_basis, transfers)

    def row_half(received, part, order):
        return pl.pallas_call(
            functools.partial(row_kernel, (owners, half_levels, tree, nodes, width, inner, per_dest)),
            in_specs=[in_smem] * 3 + [in_vmem] + [in_hbm] * 2,
            out_specs=[in_vmem] * inner,
            scratch_shapes=[pltpu.VMEM((nodes, width, part), BF16)] * 2
            + [basis_scratch, mix_scratch, pltpu.SemaphoreType.DMA((half_levels + 1,))],
            out_shape=[jax.ShapeDtypeStruct((outer, share, part), BF16)] * inner,
            compiler_params=pltpu.CompilerParams(vmem_limit_bytes=VMEM_LIMIT),
            cost_estimate=cost(part),
        )(order, col_owner, flat_ranks, received, transfers, row_basis)

    def exchange(sent):
        return lax.all_to_all(sent, "leaf", split_axis=0, concat_axis=0, tiled=True)

    def swap(partials):
        return [partials[0]] + [
            lax.ppermute(partials[e], "blk", [(i, i ^ e) for i in range(blocks)]) for e in range(1, inner)
        ]

    def sum_blocks(swapped):
        total = sum(p.astype(F32) for p in swapped).astype(BF16).reshape(outer * share, -1)
        groups = [[z * inner + x for z in range(outer)] for x in range(inner)]
        return lax.psum_scatter(total, "blk", scatter_dimension=0, tiled=True, axis_index_groups=groups)

    finished = []
    received = []
    start = 0
    for part, chunks in chunk_groups:
        order = lax.optimization_barrier((meta, sent[0]))[0] if start else meta
        sent = column_half(start, part, chunks, order)
        start += part * chunks
        for c in range(chunks):
            mine = sent[c]
            if len(received) >= IN_FLIGHT:
                mine, received[-IN_FLIGHT] = lax.optimization_barrier((mine, received[-IN_FLIGHT]))
            received.append(exchange(mine))
    order = lax.optimization_barrier((meta, sent[0]))[0]
    swapped = None
    for got in received:
        partials = list(row_half(got, got.shape[-1], order))
        order, partials[0] = lax.optimization_barrier((meta, partials[0]))
        if swapped is not None:
            swapped[0], partials[0] = lax.optimization_barrier((swapped[0], partials[0]))
            finished.append(sum_blocks(swapped))
        swapped = swap(partials)
    finished.append(sum_blocks(swapped))
    return jnp.concatenate(finished, axis=1).reshape(1, share, sides)


def solution(mesh):
    blocks = mesh.shape["blk"]
    inner = 2 ** ((blocks.bit_length() - 1) // 2)
    return jax.shard_map(
        functools.partial(local, CHUNKS, inner),
        mesh=mesh,
        in_specs=(
            P("blk", "leaf", None, None),
            P("blk", "leaf", None, None, None),
            P("blk", None, "leaf", None, None, None),
            P("blk", "leaf", None, None, None),
            P("blk", None, "leaf", None),
            P(),
            P(),
        ),
        out_specs=P("leaf", "blk", None),
        check_vma=False,
    )
```

```python
import functools

import jax
import jax.numpy as jnp
from jax import lax
from jax.experimental import pallas as pl
from jax.experimental.pallas import tpu as pltpu
from jax.sharding import PartitionSpec as P

F32 = jnp.float32
BF16 = jnp.bfloat16
VMEM_LIMIT = 56 * 2**20
UNROLL = 4
COST = 1
IN_FLIGHT = 2
DIRECT_SUMS = 1
DIRECT = 2
CHUNKS = ((128, 1), (128, 3))


def put_masked(ref, index, value, rank):
    width = value.shape[0]
    half = width // 2
    ref[(*index, slice(0, half))] = value[:half].astype(BF16)
    rows = lax.broadcasted_iota(jnp.int32, (half, value.shape[1]), 0) + half
    ref[(*index, slice(half, width))] = jnp.where(rows < rank, value[half:], 0.0).astype(BF16)


def over_trees(trees, body):
    step = min(UNROLL, trees)

    def group(g, carry):
        for u in range(step):
            body(g * step + u)
        return carry

    if step == trees:
        group(0, 0)
    else:
        lax.fori_loop(0, trees // step, group, 0)


def column_kernel(sizes, start, direct, meta, row_owner, ranks, columns_in, leaf_basis, mixings, *rest):
    owners, half_levels, tree, nodes, width = sizes
    outs, (ping, pong, cols, leaf, mix, arrived) = rest[:-6], rest[-6:]
    chips = owners // 2
    chunks = len(direct)
    firsts = [sum(owners if x else chips + 1 for x in direct[:c]) for c in range(chunks)]
    part = outs[0].shape[-1]
    trees = nodes // tree
    copies = [
        pltpu.make_async_copy(leaf_basis.at[0, 0], leaf, arrived.at[0]),
        pltpu.make_async_copy(columns_in.at[0, 0, :, pl.ds(start, cols.shape[1])], cols, arrived.at[1]),
    ] + [
        pltpu.make_async_copy(mixings.at[0, level, 0], mix.at[level], arrived.at[2 + level])
        for level in range(half_levels)
    ]
    for copy in copies:
        copy.start()
    copies[0].wait()
    copies[1].wait()

    def leaves(j):
        for n in range(tree):
            node = j * tree + n
            rows = cols[pl.ds(pl.multiple_of(node * width, width), width), :]
            value = lax.dot_general(leaf[node], rows, (((0,), (0,)), ((), ())), preferred_element_type=F32)
            put_masked(ping, (node,), value, ranks[node])

    over_trees(trees, leaves)
    now, later = ping, pong
    for level in range(1, half_levels):
        copies[1 + level].wait()
        half_i = 2 ** (level - 1)

        def mixed(j, now=now, later=later, level=level, half_i=half_i):
            for jj in range(tree // (2 * half_i)):
                for i in range(half_i):
                    first = j * tree + jj * 2 * half_i
                    x = jnp.concatenate([now[first + i], now[first + half_i + i]], axis=0)
                    n = first + 2 * i
                    t = mix[level - 1, pl.ds(n, 2)].reshape(2 * width, 2 * width)
                    value = jnp.dot(t, x, preferred_element_type=F32)
                    for e in range(2):
                        rank = ranks[level * nodes + n + e]
                        put_masked(later, (n + e,), value[e * width : (e + 1) * width], rank)

        over_trees(trees, mixed)
        now, later = later, now
    copies[1 + half_levels].wait()
    half_i = tree // 2
    pairs = half_i // owners

    def last(j):
        for d in range(owners):
            target = row_owner[meta[0] ^ d]
            for p in range(pairs):
                i = target * pairs + p
                first = j * tree + i
                x = jnp.concatenate([now[first], now[first + half_i]], axis=0)
                n = j * tree + 2 * i
                t = mix[half_levels - 1, pl.ds(n, 2)].reshape(2 * width, 2 * width)
                value = jnp.dot(t, x, preferred_element_type=F32)
                for e in range(2):
                    rank = ranks[half_levels * nodes + n + e]
                    v = value[e * width : (e + 1) * width]
                    for c in range(chunks):
                        v_c = v[:, c * part : (c + 1) * part]
                        if direct[c]:
                            put_masked(outs[firsts[c] + d], (2 * p + e, j), v_c, rank)
                        elif d % 2 == 0:
                            put_masked(outs[firsts[c] + d // 2], (2 * p + e, j), v_c, rank)
                        else:
                            put_masked(outs[firsts[c] + chips], (d // 2, 2 * p + e, j), v_c, rank)

    over_trees(trees, last)


def row_kernel(sizes, direct, relative, meta, col_owner, ranks, *rest):
    owners, half_levels, tree, nodes, width, inner, per_dest = sizes
    count = owners if direct else owners // 2 + 1
    parts, (mixings, row_basis) = rest[:count], rest[count : count + 2]
    outs, (ping, pong, basis, mix, arrived) = rest[count + 2 : -5], rest[-5:]
    trees = nodes // tree
    copies = [
        pltpu.make_async_copy(mixings.at[0, half_levels + level, 0], mix.at[level], arrived.at[level])
        for level in range(half_levels)
    ] + [pltpu.make_async_copy(row_basis.at[0, 0], basis, arrived.at[half_levels])]
    for copy in copies:
        copy.start()
    copies[0].wait()
    now, later = ping, pong
    half_j = tree // 2
    pairs = half_j // owners

    def first_mixed(p):
        for d in range(owners):
            source = col_owner[meta[0] ^ d]
            for q in range(pairs):
                n = p * tree + source * pairs + q
                if direct or d == 0:
                    x = parts[d][p, 2 * q : 2 * q + 2].reshape(2 * width, -1)
                elif d == 1:
                    x = parts[1][0, p, 2 * q : 2 * q + 2].reshape(2 * width, -1)
                else:
                    x = parts[1 + d // 2][d % 2, p, 2 * q : 2 * q + 2].reshape(2 * width, -1)
                t = jnp.concatenate([mix[0, n], mix[0, n + half_j]], axis=0)
                value = jnp.dot(t, x, preferred_element_type=F32)
                for e in range(2):
                    m = n + e * half_j
                    rank = ranks[(half_levels + 1) * nodes + m]
                    put_masked(pong, (m,), value[e * width : (e + 1) * width], rank)

    over_trees(trees, first_mixed)
    now, later = later, now
    for level in range(1, half_levels):
        copies[level].wait()
        half_j = tree // 2 ** (level + 1)

        def mixed(p, now=now, later=later, level=level, half_j=half_j):
            for i in range(2**level):
                for j in range(half_j):
                    first = p * tree + i * 2 * half_j
                    x = now[pl.ds(first + 2 * j, 2)].reshape(2 * width, -1)
                    t = jnp.concatenate([mix[level, first + j], mix[level, first + half_j + j]], axis=0)
                    value = jnp.dot(t, x, preferred_element_type=F32)
                    for e in range(2):
                        n = first + e * half_j + j
                        rank = ranks[(half_levels + 1 + level) * nodes + n]
                        put_masked(later, (n,), value[e * width : (e + 1) * width], rank)

        over_trees(trees, mixed)
        now, later = later, now
    copies[half_levels].wait()
    dests = tree // (inner * per_dest)

    def rows(p):
        for e in range(inner):
            lane = meta[1] ^ e
            for z in range(dests):
                place = p * dests + z
                if relative:
                    place = place ^ meta[2]
                for m in range(per_dest):
                    n = p * tree + (z * inner + lane) * per_dest + m
                    value = jnp.dot(basis[n], now[n], preferred_element_type=F32)
                    outs[e][place, m * width : (m + 1) * width, :] = value.astype(BF16)

    over_trees(trees, rows)


def local(chunk_groups, inner, columns_in, leaf_basis, transfers, row_basis, ranks, col_owner, row_owner):
    owners = lax.axis_size("leaf")
    chips = owners // 2
    blocks = lax.axis_size("blk")
    outer = blocks // inner
    levels = transfers.shape[1]
    half_levels = levels // 2
    nodes, width = leaf_basis.shape[2], leaf_basis.shape[4]
    sides = columns_in.shape[3]
    tree = 2**half_levels
    part_j = nodes // tree
    sub_i = tree // owners
    share = nodes * width // blocks
    per_dest = share // width
    me = lax.axis_index("leaf")
    blk = lax.axis_index("blk")
    meta = jnp.stack([me, blk % inner, blk // inner]).astype(jnp.int32)
    flat_ranks = ranks.reshape(-1)

    mix_scratch = pltpu.VMEM((half_levels, nodes, width, 2 * width), BF16)
    basis_scratch = pltpu.VMEM((nodes, width, width), BF16)
    in_hbm = pl.BlockSpec(memory_space=pl.ANY)
    in_vmem = pl.BlockSpec(memory_space=pltpu.VMEM)
    in_smem = pl.BlockSpec(memory_space=pltpu.SMEM)

    def cost(sides):
        return pl.CostEstimate(flops=int(COST * 5e7 * max(sides, 256)), bytes_accessed=int(COST * 2e7), transcendentals=0)

    def column_half(start, part, chunks, order, direct):
        total = part * chunks
        one = jax.ShapeDtypeStruct((sub_i, part_j, width, part), BF16)
        far = jax.ShapeDtypeStruct((chips, sub_i, part_j, width, part), BF16)
        outs = sum(([one] * owners if x else [one] * chips + [far] for x in direct), [])
        return pl.pallas_call(
            functools.partial(column_kernel, (owners, half_levels, tree, nodes, width), start, direct),
            in_specs=[in_smem] * 3 + [in_hbm] * 3,
            out_specs=[in_vmem] * len(outs),
            scratch_shapes=[pltpu.VMEM((nodes, width, total), BF16)] * 2
            + [
                pltpu.VMEM((nodes * width, total), BF16),
                basis_scratch,
                mix_scratch,
                pltpu.SemaphoreType.DMA((half_levels + 2,)),
            ],
            out_shape=outs,
            compiler_params=pltpu.CompilerParams(vmem_limit_bytes=VMEM_LIMIT),
            cost_estimate=cost(total),
        )(order, row_owner, flat_ranks, columns_in, leaf_basis, transfers)

    def row_half(received, part, order, direct, relative):
        return pl.pallas_call(
            functools.partial(row_kernel, (owners, half_levels, tree, nodes, width, inner, per_dest), direct, relative),
            in_specs=[in_smem] * 3 + [in_vmem] * len(received) + [in_hbm] * 2,
            out_specs=[in_vmem] * inner,
            scratch_shapes=[pltpu.VMEM((nodes, width, part), BF16)] * 2
            + [basis_scratch, mix_scratch, pltpu.SemaphoreType.DMA((half_levels + 1,))],
            out_shape=[jax.ShapeDtypeStruct((outer, share, part), BF16)] * inner,
            compiler_params=pltpu.CompilerParams(vmem_limit_bytes=VMEM_LIMIT),
            cost_estimate=cost(part),
        )(order, col_owner, flat_ranks, *received, transfers, row_basis)

    def to_mate(sent):
        return lax.ppermute(sent[chips], "leaf", [(i, i ^ 1) for i in range(owners)])

    def to_chips(sent, mate):
        moved = [
            lax.ppermute(jnp.stack([sent[y], mate[y]]), "leaf", [(i, i ^ (2 * y)) for i in range(owners)])
            for y in range(1, chips)
        ]
        return [sent[0], mate, *moved]

    def exchange(sent):
        return [sent[0]] + [
            lax.ppermute(sent[d], "leaf", [(i, i ^ d) for i in range(owners)]) for d in range(1, owners)
        ]

    def swap(partials):
        return [partials[0]] + [
            lax.ppermute(partials[e], "blk", [(i, i ^ e) for i in range(blocks)]) for e in range(1, inner)
        ]

    def add_up(terms):
        return sum(t.astype(F32) for t in terms).astype(BF16)

    def sum_blocks(swapped):
        total = add_up(swapped).reshape(outer * share, -1)
        groups = [[z * inner + x for z in range(outer)] for x in range(inner)]
        return lax.psum_scatter(total, "blk", scatter_dimension=0, tiled=True, axis_index_groups=groups)

    def sum_blocks_directly(swapped):
        total = add_up(swapped)
        return add_up(
            [total[0]]
            + [
                lax.ppermute(total[w], "blk", [(i, i ^ (w * inner)) for i in range(blocks)])
                for w in range(1, outer)
            ]
        )

    def after(value, *done):
        return lax.optimization_barrier((value, done))[0]

    sent = []
    start = 0
    for part, chunks in chunk_groups:
        direct = tuple(len(sent) + c < DIRECT for c in range(chunks))
        made = column_half(start, part, chunks, after(meta, sent[0][0]) if sent else meta, direct)
        for x in direct:
            each = owners if x else chips + 1
            sent.append(made[:each])
            made = made[each:]
        start += part * chunks
    received = [exchange(x) for x in sent[:DIRECT]]
    for c in range(DIRECT, IN_FLIGHT):
        received.append(to_chips(sent[c], to_mate(sent[c])))
    order = after(meta, sent[-1][0])
    finished = []
    swapped = None
    for c in range(len(sent)):
        partials = list(row_half(received[c], sent[c][0].shape[-1], order, c < DIRECT, c >= len(sent) - DIRECT_SUMS))
        order = after(meta, partials[0])
        if c + IN_FLIGHT < len(sent):
            following = sent[c + IN_FLIGHT]
            mate = to_mate(after(following, received[c][-1]))
            received.append(to_chips(following, after(mate, partials[0])))
        if swapped is not None:
            swapped[0] = after(swapped[0], partials[0])
            finished.append((sum_blocks_directly if c > len(sent) - DIRECT_SUMS else sum_blocks)(swapped))
        swapped = swap(partials)
    finished.append((sum_blocks_directly if DIRECT_SUMS else sum_blocks)(swapped))
    return jnp.concatenate(finished, axis=1).reshape(1, share, sides)


def solution(mesh):
    blocks = mesh.shape["blk"]
    inner = 2 ** ((blocks.bit_length() - 1) // 2)
    return jax.shard_map(
        functools.partial(local, CHUNKS, inner),
        mesh=mesh,
        in_specs=(
            P("blk", "leaf", None, None),
            P("blk", "leaf", None, None, None),
            P("blk", None, "leaf", None, None, None),
            P("blk", "leaf", None, None, None),
            P("blk", None, "leaf", None),
            P(),
            P(),
        ),
        out_specs=P("leaf", "blk", None),
        check_vma=False,
    )
```

```python
import functools

import jax
import jax.numpy as jnp
from jax import lax
from jax.experimental import pallas as pl
from jax.experimental.pallas import tpu as pltpu
from jax.sharding import PartitionSpec as P

F32 = jnp.float32
BF16 = jnp.bfloat16
VMEM_LIMIT = 56 * 2**20
UNROLL = 4
COST = 1
IN_FLIGHT = 2
SUMS = ("far first", "offloaded", "offloaded", "permuted")
DIRECT = 2
CHUNKS = ((128, 1), (128, 3))


def put_masked(ref, index, value, rank):
    width = value.shape[0]
    half = width // 2
    ref[(*index, slice(0, half))] = value[:half].astype(BF16)
    rows = lax.broadcasted_iota(jnp.int32, (half, value.shape[1]), 0) + half
    ref[(*index, slice(half, width))] = jnp.where(rows < rank, value[half:], 0.0).astype(BF16)


def over_trees(trees, body):
    step = min(UNROLL, trees)

    def group(g, carry):
        for u in range(step):
            body(g * step + u)
        return carry

    if step == trees:
        group(0, 0)
    else:
        lax.fori_loop(0, trees // step, group, 0)


def column_kernel(sizes, start, direct, meta, row_owner, ranks, columns_in, leaf_basis, mixings, *rest):
    owners, half_levels, tree, nodes, width = sizes
    outs, (ping, pong, cols, leaf, mix, arrived) = rest[:-6], rest[-6:]
    chips = owners // 2
    chunks = len(direct)
    firsts = [sum(owners if x else chips + 1 for x in direct[:c]) for c in range(chunks)]
    part = outs[0].shape[-1]
    trees = nodes // tree
    copies = [
        pltpu.make_async_copy(leaf_basis.at[0, 0], leaf, arrived.at[0]),
        pltpu.make_async_copy(columns_in.at[0, 0, :, pl.ds(start, cols.shape[1])], cols, arrived.at[1]),
    ] + [
        pltpu.make_async_copy(mixings.at[0, level, 0], mix.at[level], arrived.at[2 + level])
        for level in range(half_levels)
    ]
    for copy in copies:
        copy.start()
    copies[0].wait()
    copies[1].wait()

    def leaves(j):
        for n in range(tree):
            node = j * tree + n
            rows = cols[pl.ds(pl.multiple_of(node * width, width), width), :]
            value = lax.dot_general(leaf[node], rows, (((0,), (0,)), ((), ())), preferred_element_type=F32)
            put_masked(ping, (node,), value, ranks[node])

    over_trees(trees, leaves)
    now, later = ping, pong
    for level in range(1, half_levels):
        copies[1 + level].wait()
        half_i = 2 ** (level - 1)

        def mixed(j, now=now, later=later, level=level, half_i=half_i):
            for jj in range(tree // (2 * half_i)):
                for i in range(half_i):
                    first = j * tree + jj * 2 * half_i
                    x = jnp.concatenate([now[first + i], now[first + half_i + i]], axis=0)
                    n = first + 2 * i
                    t = mix[level - 1, pl.ds(n, 2)].reshape(2 * width, 2 * width)
                    value = jnp.dot(t, x, preferred_element_type=F32)
                    for e in range(2):
                        rank = ranks[level * nodes + n + e]
                        put_masked(later, (n + e,), value[e * width : (e + 1) * width], rank)

        over_trees(trees, mixed)
        now, later = later, now
    copies[1 + half_levels].wait()
    half_i = tree // 2
    pairs = half_i // owners

    def last(j):
        for d in range(owners):
            target = row_owner[meta[0] ^ d]
            for p in range(pairs):
                i = target * pairs + p
                first = j * tree + i
                x = jnp.concatenate([now[first], now[first + half_i]], axis=0)
                n = j * tree + 2 * i
                t = mix[half_levels - 1, pl.ds(n, 2)].reshape(2 * width, 2 * width)
                value = jnp.dot(t, x, preferred_element_type=F32)
                for e in range(2):
                    rank = ranks[half_levels * nodes + n + e]
                    v = value[e * width : (e + 1) * width]
                    for c in range(chunks):
                        v_c = v[:, c * part : (c + 1) * part]
                        if direct[c]:
                            put_masked(outs[firsts[c] + d], (2 * p + e, j), v_c, rank)
                        elif d % 2 == 0:
                            put_masked(outs[firsts[c] + d // 2], (2 * p + e, j), v_c, rank)
                        else:
                            put_masked(outs[firsts[c] + chips], (d // 2, 2 * p + e, j), v_c, rank)

    over_trees(trees, last)


def row_kernel(sizes, direct, how, meta, col_owner, ranks, *rest):
    owners, half_levels, tree, nodes, width, inner, per_dest = sizes
    count = owners if direct else owners // 2 + 1
    parts, (mixings, row_basis) = rest[:count], rest[count : count + 2]
    outs, (ping, pong, basis, mix, arrived) = rest[count + 2 : -5], rest[-5:]
    trees = nodes // tree
    copies = [
        pltpu.make_async_copy(mixings.at[0, half_levels + level, 0], mix.at[level], arrived.at[level])
        for level in range(half_levels)
    ] + [pltpu.make_async_copy(row_basis.at[0, 0], basis, arrived.at[half_levels])]
    for copy in copies:
        copy.start()
    copies[0].wait()
    now, later = ping, pong
    half_j = tree // 2
    pairs = half_j // owners

    def first_mixed(p):
        for d in range(owners):
            source = col_owner[meta[0] ^ d]
            for q in range(pairs):
                n = p * tree + source * pairs + q
                if direct or d == 0:
                    x = parts[d][p, 2 * q : 2 * q + 2].reshape(2 * width, -1)
                elif d == 1:
                    x = parts[1][0, p, 2 * q : 2 * q + 2].reshape(2 * width, -1)
                else:
                    x = parts[1 + d // 2][d % 2, p, 2 * q : 2 * q + 2].reshape(2 * width, -1)
                t = jnp.concatenate([mix[0, n], mix[0, n + half_j]], axis=0)
                value = jnp.dot(t, x, preferred_element_type=F32)
                for e in range(2):
                    m = n + e * half_j
                    rank = ranks[(half_levels + 1) * nodes + m]
                    put_masked(pong, (m,), value[e * width : (e + 1) * width], rank)

    over_trees(trees, first_mixed)
    now, later = later, now
    for level in range(1, half_levels):
        copies[level].wait()
        half_j = tree // 2 ** (level + 1)

        def mixed(p, now=now, later=later, level=level, half_j=half_j):
            for i in range(2**level):
                for j in range(half_j):
                    first = p * tree + i * 2 * half_j
                    x = now[pl.ds(first + 2 * j, 2)].reshape(2 * width, -1)
                    t = jnp.concatenate([mix[level, first + j], mix[level, first + half_j + j]], axis=0)
                    value = jnp.dot(t, x, preferred_element_type=F32)
                    for e in range(2):
                        n = first + e * half_j + j
                        rank = ranks[(half_levels + 1 + level) * nodes + n]
                        put_masked(later, (n,), value[e * width : (e + 1) * width], rank)

        over_trees(trees, mixed)
        now, later = later, now
    copies[half_levels].wait()
    dests = tree // (inner * per_dest)

    def rows(p):
        for e in range(inner):
            lane = meta[1] ^ e
            for z in range(dests):
                place = p * dests + z
                if how == "permuted":
                    place = place ^ meta[2]
                for m in range(per_dest):
                    n = p * tree + (z * inner + lane) * per_dest + m
                    value = jnp.dot(basis[n], now[n], preferred_element_type=F32)
                    span = slice(m * width, (m + 1) * width)
                    if how == "far first":
                        outs[0][place, e, span, :] = value.astype(BF16)
                    else:
                        outs[e][place, span, :] = value.astype(BF16)

    over_trees(trees, rows)


def local(chunk_groups, inner, columns_in, leaf_basis, transfers, row_basis, ranks, col_owner, row_owner):
    owners = lax.axis_size("leaf")
    chips = owners // 2
    blocks = lax.axis_size("blk")
    outer = blocks // inner
    levels = transfers.shape[1]
    half_levels = levels // 2
    nodes, width = leaf_basis.shape[2], leaf_basis.shape[4]
    sides = columns_in.shape[3]
    tree = 2**half_levels
    part_j = nodes // tree
    sub_i = tree // owners
    share = nodes * width // blocks
    per_dest = share // width
    me = lax.axis_index("leaf")
    blk = lax.axis_index("blk")
    meta = jnp.stack([me, blk % inner, blk // inner]).astype(jnp.int32)
    flat_ranks = ranks.reshape(-1)

    mix_scratch = pltpu.VMEM((half_levels, nodes, width, 2 * width), BF16)
    basis_scratch = pltpu.VMEM((nodes, width, width), BF16)
    in_hbm = pl.BlockSpec(memory_space=pl.ANY)
    in_vmem = pl.BlockSpec(memory_space=pltpu.VMEM)
    in_smem = pl.BlockSpec(memory_space=pltpu.SMEM)

    def cost(sides):
        return pl.CostEstimate(flops=int(COST * 5e7 * max(sides, 256)), bytes_accessed=int(COST * 2e7), transcendentals=0)

    def column_half(start, part, chunks, order, direct):
        total = part * chunks
        one = jax.ShapeDtypeStruct((sub_i, part_j, width, part), BF16)
        far = jax.ShapeDtypeStruct((chips, sub_i, part_j, width, part), BF16)
        outs = sum(([one] * owners if x else [one] * chips + [far] for x in direct), [])
        return pl.pallas_call(
            functools.partial(column_kernel, (owners, half_levels, tree, nodes, width), start, direct),
            in_specs=[in_smem] * 3 + [in_hbm] * 3,
            out_specs=[in_vmem] * len(outs),
            scratch_shapes=[pltpu.VMEM((nodes, width, total), BF16)] * 2
            + [
                pltpu.VMEM((nodes * width, total), BF16),
                basis_scratch,
                mix_scratch,
                pltpu.SemaphoreType.DMA((half_levels + 2,)),
            ],
            out_shape=outs,
            compiler_params=pltpu.CompilerParams(vmem_limit_bytes=VMEM_LIMIT),
            cost_estimate=cost(total),
        )(order, row_owner, flat_ranks, columns_in, leaf_basis, transfers)

    def row_half(received, part, order, direct, how):
        outs = [jax.ShapeDtypeStruct((outer, share, part), BF16)] * inner
        if how == "far first":
            outs = [jax.ShapeDtypeStruct((outer, inner, share, part), BF16)]
        return pl.pallas_call(
            functools.partial(row_kernel, (owners, half_levels, tree, nodes, width, inner, per_dest), direct, how),
            in_specs=[in_smem] * 3 + [in_vmem] * len(received) + [in_hbm] * 2,
            out_specs=[in_vmem] * len(outs),
            scratch_shapes=[pltpu.VMEM((nodes, width, part), BF16)] * 2
            + [basis_scratch, mix_scratch, pltpu.SemaphoreType.DMA((half_levels + 1,))],
            out_shape=outs,
            compiler_params=pltpu.CompilerParams(vmem_limit_bytes=VMEM_LIMIT),
            cost_estimate=cost(part),
        )(order, col_owner, flat_ranks, *received, transfers, row_basis)

    def to_mate(sent):
        return lax.ppermute(sent[chips], "leaf", [(i, i ^ 1) for i in range(owners)])

    def to_chips(sent, mate):
        moved = [
            lax.ppermute(jnp.stack([sent[y], mate[y]]), "leaf", [(i, i ^ (2 * y)) for i in range(owners)])
            for y in range(1, chips)
        ]
        return [sent[0], mate, *moved]

    def exchange(sent):
        return [sent[0]] + [
            lax.ppermute(sent[d], "leaf", [(i, i ^ d) for i in range(owners)]) for d in range(1, owners)
        ]

    def swap(partials):
        return [partials[0]] + [
            lax.ppermute(partials[e], "blk", [(i, i ^ e) for i in range(blocks)]) for e in range(1, inner)
        ]

    def add_up(terms):
        return sum(t.astype(F32) for t in terms).astype(BF16)

    def far_sum(terms):
        groups = [[z * inner + x for z in range(outer)] for x in range(inner)]
        return lax.psum_scatter(terms, "blk", scatter_dimension=0, tiled=True, axis_index_groups=groups)

    def sum_blocks(swapped, how):
        total = add_up(swapped)
        if how == "offloaded":
            return far_sum(total.reshape(outer * share, -1))
        steps = range(1, outer)
        moved = [lax.ppermute(total[w], "blk", [(i, i ^ (w * inner)) for i in range(blocks)]) for w in steps]
        return add_up([total[0], *moved])

    def after(value, *done):
        return lax.optimization_barrier((value, done))[0]

    sent = []
    start = 0
    for part, chunks in chunk_groups:
        direct = tuple(len(sent) + c < DIRECT for c in range(chunks))
        made = column_half(start, part, chunks, after(meta, sent[0][0]) if sent else meta, direct)
        for x in direct:
            each = owners if x else chips + 1
            sent.append(made[:each])
            made = made[each:]
        start += part * chunks
    received = [exchange(x) for x in sent[:DIRECT]]
    for c in range(DIRECT, IN_FLIGHT):
        received.append(to_chips(sent[c], to_mate(sent[c])))
    order = after(meta, sent[-1][0])
    finished = {}
    waiting = None
    early = None
    for c in range(len(sent)):
        how = SUMS[c % len(SUMS)]
        partials = list(row_half(received[c], sent[c][0].shape[-1], order, c < DIRECT, how))
        order = after(meta, partials[0])
        if c + IN_FLIGHT < len(sent):
            following = sent[c + IN_FLIGHT]
            mate = to_mate(after(following, received[c][-1]))
            received.append(to_chips(following, after(mate, partials[0])))
        if waiting is not None:
            last, swapped, manner = waiting
            if early is not None and c == len(sent) - 1:
                finished[0] = add_up(swap(early))
                swapped[0] = after(swapped[0], partials[0], finished[0])
            else:
                swapped[0] = after(swapped[0], partials[0])
            finished[last] = sum_blocks(swapped, manner)
        if how == "far first":
            early = far_sum(after(partials[0], *received[1][1:]).reshape(outer, -1, partials[0].shape[-1])).reshape(inner, share, -1)
        else:
            waiting = (c, swap(partials), how)
    last, swapped, manner = waiting
    finished[last] = sum_blocks(swapped, manner)
    finished = [finished[c] for c in range(len(sent))]
    return jnp.concatenate(finished, axis=1).reshape(1, share, sides)


def solution(mesh):
    blocks = mesh.shape["blk"]
    inner = 2 ** ((blocks.bit_length() - 1) // 2)
    return jax.shard_map(
        functools.partial(local, CHUNKS, inner),
        mesh=mesh,
        in_specs=(
            P("blk", "leaf", None, None),
            P("blk", "leaf", None, None, None),
            P("blk", None, "leaf", None, None, None),
            P("blk", "leaf", None, None, None),
            P("blk", None, "leaf", None),
            P(),
            P(),
        ),
        out_specs=P("leaf", "blk", None),
        check_vma=False,
    )
```
